32 devices in a mesh: pair: 8 (over z, x), virt: 4 (over y, core).
Axes of the slice: x: 2, y: 2, z: 4, core: 2. Of those that a mesh axis runs over, the one named last changes fastest.
Arguments:
- t_amps: bfloat16 [4096, 1024], P('pair', 'virt'), may hold values from -6 to 6
- v_ints: bfloat16 [4096, 1024], P('virt', 'pair'), may hold values from -0.1875 to 0.1875
- t_mask: int32 [32, 8], P('pair', 'virt'), may hold values 0 or 1
- v_mask: int32 [32, 8], P('virt'), may hold values from 0 to 1, as said below
Outputs:
- ladder: bfloat16 [4096, 4096], P('pair', 'virt')
The draws below stay inside these ranges and needn't reach their ends.
Inputs may be any that keep to these rules, and one draw needn't show every extreme that they name: `v_mask`: in each column and each aligned block of 8 rows (one device's ab tiles) between 1 and 4 entries are 1; in every column some block has exactly 4.
All inputs are finite; a program needn't handle non-finite values. No bound on the sum of `t_mask` on one device may be relied on, other than what follows from the above.
Results may differ from the reference program's by a relative error of at most 0.001.
Values may be sent and summed in bfloat16 or wider, within the bound.
A program may use at most 64 MiB of HBM per device.

```python
import jax
import jax.numpy as jnp
from jax import lax

TILE = 128
PAIR_DEV = 512
NPAIR = 4096
AB = 4096
KCD = 1024
PT = 32
ABT = 32
KT = 8
ABT_DEV = 8
VCAP = 4
N_PAIR = 8
N_VIRT = 4


def draw_v_mask(key, part):
    base = jax.random.fold_in(key, 17)
    counts = jax.random.randint(jax.random.fold_in(base, 1), (N_VIRT, KT), 1, VCAP + 1)
    forced = jax.random.randint(jax.random.fold_in(base, 2), (KT,), 0, N_VIRT)
    rows_v = jnp.arange(N_VIRT, dtype=jnp.int32)[:, None]
    counts = jnp.where(rows_v == forced[None, :], VCAP, counts)
    keys = jax.random.split(jax.random.fold_in(base, 3), N_VIRT * KT)
    ranks = jax.vmap(lambda single: jax.random.permutation(single, ABT_DEV))(keys)
    ranks = ranks.reshape(N_VIRT, KT, ABT_DEV)
    ones = (ranks < counts[:, :, None]).astype(jnp.int32)
    return jnp.transpose(ones, (0, 2, 1)).reshape(ABT, KT)


def touch_ends(entries, rng, least, top_value):
    longest = entries.shape.index(max(entries.shape))
    spots = []
    for shift in (0, 1):
        where = [jax.random.randint(jax.random.fold_in(rng, axis), (), 0, length) for axis, length in enumerate(entries.shape)]
        where[longest] = (where[longest] + shift) % entries.shape[longest]
        spots.append(tuple(where))
    return entries.at[spots[0]].set(least).at[spots[1]].set(top_value)


def steps_of(key, extent, cuts, least, largest):
    def one(axis_at, shards_of):
        steps = jax.random.uniform(jax.random.fold_in(jax.random.fold_in(key, 6), axis_at), (shards_of,), jnp.float32, least / len(cuts), largest / len(cuts))
        return jnp.repeat(jnp.exp(steps), extent[axis_at] // shards_of).reshape((-1,) + (1,) * (len(extent) - axis_at - 1))

    level = one(*cuts[0])
    for cut in cuts[1:]:
        level = level * one(*cut)
    return level


def gaussian(own_key, shape, spread, limit, cuts=(), kind=jnp.bfloat16):
    loudness = steps_of(own_key, shape, cuts, -0.22, 0.18) if cuts else 1.0
    array = jax.random.normal(own_key, shape, jnp.float32) * spread * loudness
    return jnp.minimum(jnp.maximum(array, -limit), limit).astype(kind)


def setup_inputs(seed: int = 0) -> dict:
    arg_keys = jax.random.split(jax.random.key(seed), 5)
    return {
        "t_amps": gaussian(arg_keys[0], (NPAIR, KCD), 1.0, 6.0, ((0, 8), (1, 4))),
        "v_ints": gaussian(arg_keys[1], (AB, KCD), KCD ** -0.5, 0.1875, ((0, 4), (1, 8))),
        "t_mask": touch_ends((jax.random.randint(arg_keys[2], (PT, KT), 0, 4) < 3).astype(jnp.int32), jax.random.fold_in(arg_keys[2], 1), 0, 1),
        "v_mask": draw_v_mask(jax.random.fold_in(arg_keys[4], 71), 0),
    }


def expand(mask):
    return jnp.repeat(jnp.repeat(mask, TILE, axis=0), TILE, axis=1).astype(jnp.bfloat16)


def reference(t_amps, v_ints, t_mask, v_mask):
    masked_t = t_amps * expand(t_mask)
    masked_v = v_ints * expand(v_mask)
    blocks = masked_t.reshape(N_PAIR, PAIR_DEV, KCD)

    def one_block(rows):
        return lax.dot_general(rows, masked_v, (((1,), (1,)), ((), ())), preferred_element_type=jnp.float32).astype(jnp.bfloat16)

    return lax.map(one_block, blocks).reshape(NPAIR, AB)
```

```python
import functools

import jax
import jax.numpy as jnp
from jax import lax
from jax.experimental import pallas as pl
from jax.experimental.pallas import tpu as pltpu
from jax.sharding import PartitionSpec as P

TILE = 128
VCAP = 4
NT = 256
MESH = pl.DeviceIdType.MESH


def nth_nearest(s, z, Z):
    low = jnp.minimum(z, Z - 1 - z)
    near = z - (s + 1) // 2 if s % 2 else z + s // 2
    far = jnp.where(z < Z - 1 - z, s, Z - 1 - s)
    return jnp.where(s <= 2 * low, near, far)


def kernel(
    Z, H, tm_ref, vm_ref, t_hbm, v_hbm, out_ref,
    t_in, v_in, tf, vc, stage, vd, acc,
    in_sem, v_recv, v_send, t_recv, t_far, t_near,
):
    ab_tiles = vm_ref.shape[0]
    me = lax.axis_index("pair")
    my_q = lax.axis_index("virt")
    z, x = me // 2, me % 2
    h, c = my_q // 2, my_q % 2
    up, down, side = me + 2, me - 2, 2 * z + (1 - x)
    sibling = 2 * h + (1 - c)

    load_v = pltpu.make_async_copy(v_hbm, v_in, in_sem.at[0])
    load_t = pltpu.make_async_copy(t_hbm, t_in, in_sem.at[1])
    load_v.start()
    load_t.start()

    barrier = pltpu.get_barrier_semaphore()

    def greet(pair, virt):
        pl.semaphore_signal(barrier, inc=1, device_id=(pair, virt), device_id_type=MESH)

    @pl.when(z > 0)
    def _():
        greet(down, my_q)

    @pl.when(z < Z - 1)
    def _():
        greet(up, my_q)

    greet(side, my_q)
    greet(me, sibling)
    for i in range(1, H):
        greet(me, 2 * lax.rem(h + i, H) + c)

    load_v.wait()
    seen = jnp.int32(0)
    picks = [jnp.int32(0)] * VCAP
    for i in range(ab_tiles):
        flag = vm_ref[i, me]
        for j in range(VCAP):
            picks[j] = jnp.where((flag != 0) & (seen == j), i, picks[j])
        seen = seen + flag
    for j in range(VCAP):
        vc[me, j] = v_in[picks[j]]

    pl.semaphore_wait(
        barrier,
        1 + H + jnp.where(z > 0, 1, 0) + jnp.where(z < Z - 1, 1, 0),
    )

    def v_copy(block, way, to):
        return pltpu.make_async_remote_copy(
            src_ref=vc.at[block],
            dst_ref=vc.at[block],
            send_sem=v_send.at[way, block],
            recv_sem=v_recv.at[block],
            device_id=(to, my_q),
            device_id_type=MESH,
        )

    def t_copy(block, sem, to):
        return pltpu.make_async_remote_copy(
            src_ref=tf.at[block],
            dst_ref=tf.at[block],
            send_sem=sem,
            recv_sem=t_recv.at[block],
            device_id=(me, to),
            device_id_type=MESH,
        )

    def pass_on(a):
        block = 2 * a + x

        @pl.when((a <= z) & (z < Z - 1))
        def _():
            v_copy(block, 0, up).start()

        @pl.when((a >= z) & (z > 0))
        def _():
            v_copy(block, 1, down).start()

        v_copy(block, 2, side).start()

    pass_on(z)

    load_t.wait()
    cd = tm_ref.shape[0]
    for i in range(tm_ref.shape[1]):
        for j in range(cd):
            rows, cols = pl.ds(i * TILE, TILE), pl.ds(j * TILE, TILE)
            flag = jnp.full((TILE, TILE), tm_ref[j, i].astype(jnp.float32))
            tf[my_q, rows, cols] = t_in[rows, cols] * flag.astype(jnp.bfloat16)
    for i in range(1, H):
        t_copy(my_q, t_far.at[i], 2 * lax.rem(h + i, H) + c).start()
    t_copy(my_q, t_near.at[my_q], sibling).start()

    stage[VCAP] = jnp.zeros((TILE, TILE), jnp.bfloat16)

    def expand(a):
        for j in range(2):
            k = 2 * a + j
            for i in range(VCAP):
                stage[i] = vc[k, i]
            rank = jnp.int32(0)
            for i in range(ab_tiles):
                flag = vm_ref[i, k]
                where = jnp.where(flag != 0, rank, VCAP)
                rank = rank + flag
                vd[pl.ds(i * TILE, TILE), pl.ds(j * TILE, TILE)] = stage[where]

    def multiply(a, s):
        expand(a)
        left = tf.at[a]

        @pl.loop(0, ab_tiles * TILE // NT)
        def _(n):
            cols = pl.ds(pl.multiple_of(n * NT, NT), NT)
            part = lax.dot_general(
                left[...], vd[cols, :], (((1,), (1,)), ((), ())),
                preferred_element_type=jnp.float32,
            )
            if s > 0:
                part = part + acc[:, cols]
            if s < Z - 1:
                acc[:, cols] = part
            else:
                out_ref[:, cols] = part.astype(out_ref.dtype)

    def take(s):
        a = nth_nearest(s, z, Z)
        v_copy(2 * a + x, 2, side).wait_recv()
        pass_on(a)

    def finish(s):
        a = nth_nearest(s, z, Z)
        v_copy(2 * a + (1 - x), 2, side).wait_recv()
        multiply(a, s)

    first = min(2, Z - 1)
    for s in range(1, first + 1):
        take(s)
    for i in range(1, H):
        block = 2 * lax.rem(h + H - i, H) + c
        t_copy(block, t_far.at[i], sibling).wait_recv()
        t_copy(block, t_near.at[block], sibling).start()
    for i in range(H):
        block = 2 * i + (1 - c)
        t_copy(block, t_near.at[block], sibling).wait_recv()
    for s in range(Z):
        if s > first:
            take(s)
        if s >= first:
            finish(s - first)
    for s in range(Z - first, Z):
        finish(s)

    for s in range(Z):
        a = nth_nearest(s, z, Z)
        block = 2 * a + x

        @pl.when((a <= z) & (z < Z - 1))
        def _():
            v_copy(block, 0, up).wait_send()

        @pl.when((a >= z) & (z > 0))
        def _():
            v_copy(block, 1, down).wait_send()

        v_copy(block, 2, side).wait_send()
    for i in range(1, H):
        t_copy(my_q, t_far.at[i], sibling).wait_send()
    for i in range(H):
        block = 2 * i + c
        t_copy(block, t_near.at[block], sibling).wait_send()


def local(n_pair, n_virt, t_amps, v_ints, t_mask, v_mask):
    rows, t_cols = t_amps.shape
    ab_rows, _ = v_ints.shape
    ab_tiles = ab_rows // TILE
    dma = pltpu.SemaphoreType.DMA
    bf16 = jnp.bfloat16
    return pl.pallas_call(
        functools.partial(kernel, n_pair // 2, n_virt // 2),
        out_shape=jax.ShapeDtypeStruct((rows, ab_rows), bf16),
        in_specs=[pl.BlockSpec(memory_space=pltpu.SMEM)] * 2
        + [pl.BlockSpec(memory_space=pl.ANY)] * 2,
        out_specs=pl.BlockSpec(memory_space=pltpu.VMEM),
        scratch_shapes=[
            pltpu.VMEM((rows, t_cols), bf16),
            pltpu.VMEM((ab_tiles, TILE, TILE), bf16),
            pltpu.VMEM((n_virt, rows, t_cols), bf16),
            pltpu.VMEM((n_pair, VCAP, TILE, TILE), bf16),
            pltpu.VMEM((VCAP + 1, TILE, TILE), bf16),
            pltpu.VMEM((ab_rows, 2 * TILE), bf16),
            pltpu.VMEM((rows, ab_rows), jnp.float32),
            dma((2,)),
            dma((n_pair,)),
            dma((3, n_pair)),
            dma((n_virt,)),
            dma((n_virt,)),
            dma((n_virt,)),
        ],
        compiler_params=pltpu.CompilerParams(
            collective_id=0, has_side_effects=True, vmem_limit_bytes=40 * 2**20
        ),
    )(t_mask.T, v_mask, t_amps, v_ints.reshape(ab_tiles, TILE, TILE))


def solution(mesh):
    return jax.shard_map(
        functools.partial(local, mesh.shape["pair"], mesh.shape["virt"]),
        mesh=mesh,
        in_specs=(P("pair", "virt"), P("virt", "pair"), P("pair", "virt"), P("virt", None)),
        out_specs=P("pair", "virt"),
        check_vma=False,
    )
```

```python
import functools

import jax
import jax.numpy as jnp
from jax import lax
from jax.experimental import pallas as pl
from jax.experimental.pallas import tpu as pltpu
from jax.sharding import PartitionSpec as P

TILE = 128
VCAP = 4
CHUNKS = 2
WINDOW = 3
NT = 256
MESH = pl.DeviceIdType.MESH


def nth_nearest(s, z, Z):
    low = jnp.minimum(z, Z - 1 - z)
    near = z - (s + 1) // 2 if s % 2 else z + s // 2
    far = jnp.where(z < Z - 1 - z, s, Z - 1 - s)
    return jnp.where(s <= 2 * low, near, far)


def kernel(
    Z, H, tm_hbm, vm_hbm, t_hbm, v_hbm, out_ref,
    tm_ref, vm_ref, t_in, v_in, tf, vc, stage, vd, acc,
    in_sem, v_recv, v_send, t_recv, t_far, t_near,
):
    ab_tiles = vm_ref.shape[0]
    me = lax.axis_index("pair")
    my_q = lax.axis_index("virt")
    z, x = me // 2, me % 2
    h, c = my_q // 2, my_q % 2
    up, down, side = me + 2, me - 2, 2 * z + (1 - x)
    sibling = 2 * h + (1 - c)

    load_v = pltpu.make_async_copy(v_hbm, v_in, in_sem.at[0])
    load_t = pltpu.make_async_copy(t_hbm, t_in, in_sem.at[1])
    load_vm = pltpu.make_async_copy(vm_hbm, vm_ref, in_sem.at[2])
    load_tm = pltpu.make_async_copy(tm_hbm, tm_ref, in_sem.at[3])
    load_vm.start()
    load_v.start()
    load_tm.start()
    load_t.start()

    barrier = pltpu.get_barrier_semaphore()

    def greet(pair, virt):
        pl.semaphore_signal(barrier, inc=1, device_id=(pair, virt), device_id_type=MESH)

    @pl.when(z > 0)
    def _():
        greet(down, my_q)

    @pl.when(z < Z - 1)
    def _():
        greet(up, my_q)

    greet(side, my_q)
    greet(me, sibling)
    for i in range(1, H):
        greet(me, 2 * lax.rem(h + i, H) + c)

    load_vm.wait()
    seen = jnp.int32(0)
    picks = [jnp.int32(0)] * VCAP
    for i in range(ab_tiles):
        flag = vm_ref[i, me]
        for j in range(VCAP):
            picks[j] = jnp.where((flag != 0) & (seen == j), i, picks[j])
        seen = seen + flag
    load_v.wait()
    for j in range(VCAP):
        vc[me, j] = v_in[picks[j]]

    pl.semaphore_wait(
        barrier,
        1 + H + jnp.where(z > 0, 1, 0) + jnp.where(z < Z - 1, 1, 0),
    )

    def v_copy(block, u, way, to):
        part = pl.ds(u * (VCAP // CHUNKS), VCAP // CHUNKS)
        return pltpu.make_async_remote_copy(
            src_ref=vc.at[block, part],
            dst_ref=vc.at[block, part],
            send_sem=v_send.at[way, block, u],
            recv_sem=v_recv.at[block, u],
            device_id=(to, my_q),
            device_id_type=MESH,
        )

    def t_copy(block, sem, to):
        return pltpu.make_async_remote_copy(
            src_ref=tf.at[block],
            dst_ref=tf.at[block],
            send_sem=sem,
            recv_sem=t_recv.at[block],
            device_id=(me, to),
            device_id_type=MESH,
        )

    def stream(way, s):
        if way == 0:
            return z - s, (z >= s) & (z < Z - 1), up
        if way == 1:
            return z + s, (z + s < Z) & (z > 0), down
        return nth_nearest(s, z, Z), None, side

    def each(way, n, act):
        a, there, to = stream(way, n // CHUNKS)
        copy = v_copy(2 * a + x, n % CHUNKS, way, to)
        if there is None:
            act(copy)
        else:
            pl.when(there)(lambda: act(copy))

    def start(copy):
        copy.start()

    def wait_send(copy):
        copy.wait_send()

    def drain(way, n):
        there = stream(way, n // CHUNKS)[1]
        if there is None:
            if n + WINDOW >= Z * CHUNKS:
                each(way, n, wait_send)
        elif n + WINDOW >= Z * CHUNKS:
            each(way, n, wait_send)
        else:
            later = stream(way, (n + WINDOW) // CHUNKS)[1]

            @pl.when(jnp.logical_not(later))
            def _():
                each(way, n, wait_send)

    def tick(n):
        s, u = n // CHUNKS, n % CHUNKS
        if s > 0:

            @pl.when(z >= s)
            def _():
                v_copy(2 * (z - s) + x, u, 0, side).wait_recv()

            @pl.when(z + s < Z)
            def _():
                v_copy(2 * (z + s) + x, u, 0, side).wait_recv()

        for way in range(3):
            if n >= WINDOW:
                a, there, to = stream(way, s)
                if there is None:
                    each(way, n - WINDOW, wait_send)
                else:
                    pl.when(there)(lambda: each(way, n - WINDOW, wait_send))
            each(way, n, start)

    for n in range(WINDOW):
        tick(n)

    load_tm.wait()
    load_t.wait()
    cd = tm_ref.shape[0]
    for i in range(tm_ref.shape[1]):
        for j in range(cd):
            rows, cols = pl.ds(i * TILE, TILE), pl.ds(j * TILE, TILE)
            flag = jnp.full((TILE, TILE), tm_ref[j, i].astype(jnp.float32))
            tf[my_q, rows, cols] = t_in[rows, cols] * flag.astype(jnp.bfloat16)
    for i in range(1, H):
        t_copy(my_q, t_far.at[i], 2 * lax.rem(h + i, H) + c).start()
    t_copy(my_q, t_near.at[my_q], sibling).start()

    stage[VCAP] = jnp.zeros((TILE, TILE), jnp.bfloat16)

    def expand(a):
        for j in range(2):
            k = 2 * a + j
            for i in range(VCAP):
                stage[i] = vc[k, i]
            rank = jnp.int32(0)
            for i in range(ab_tiles):
                flag = vm_ref[i, k]
                where = jnp.where(flag != 0, rank, VCAP)
                rank = rank + flag
                vd[pl.ds(i * TILE, TILE), pl.ds(j * TILE, TILE)] = stage[where]

    def multiply(a, s):
        expand(a)
        left = tf.at[a]

        @pl.loop(0, ab_tiles * TILE // NT)
        def _(n):
            cols = pl.ds(pl.multiple_of(n * NT, NT), NT)
            part = lax.dot_general(
                left[...], vd[cols, :], (((1,), (1,)), ((), ())),
                preferred_element_type=jnp.float32,
            )
            if s > 0:
                part = part + acc[:, cols]
            if s < Z - 1:
                acc[:, cols] = part
            else:
                out_ref[:, cols] = part.astype(out_ref.dtype)

    def finish(s):
        a = nth_nearest(s, z, Z)
        for u in range(CHUNKS):
            v_copy(2 * a + (1 - x), u, 2, side).wait_recv()
        multiply(a, s)

    def t_onward():
        for i in range(1, H):
            block = 2 * lax.rem(h + H - i, H) + c
            t_copy(block, t_far.at[i], sibling).wait_recv()
            t_copy(block, t_near.at[block], sibling).start()

    def t_arrived():
        for i in range(H):
            block = 2 * i + (1 - c)
            t_copy(block, t_near.at[block], sibling).wait_recv()

    done = 0
    last = (Z - 1) * CHUNKS
    for n in range(WINDOW, Z * CHUNKS):
        tick(n)
        if n == last:
            t_onward()
        if n == last + 1:
            t_arrived()
        if n >= last + 1 and done < Z - 1:
            finish(done)
            done += 1
    for s in range(done, Z):
        finish(s)

    for n in range(Z * CHUNKS):
        for way in range(3):
            drain(way, n)
    for i in range(1, H):
        t_copy(my_q, t_far.at[i], sibling).wait_send()
    for i in range(H):
        block = 2 * i + c
        t_copy(block, t_near.at[block], sibling).wait_send()


def local(n_pair, n_virt, t_amps, v_ints, t_mask, v_mask):
    rows, t_cols = t_amps.shape
    ab_rows, _ = v_ints.shape
    ab_tiles = ab_rows // TILE
    dma = pltpu.SemaphoreType.DMA
    bf16 = jnp.bfloat16
    return pl.pallas_call(
        functools.partial(kernel, n_pair // 2, n_virt // 2),
        out_shape=pltpu.VMEM((rows, ab_rows), bf16),
        in_specs=[pl.BlockSpec(memory_space=pl.ANY)] * 4,
        out_specs=pl.BlockSpec(memory_space=pltpu.VMEM),
        scratch_shapes=[
            pltpu.SMEM(t_mask.shape[::-1], jnp.int32),
            pltpu.SMEM(v_mask.shape, jnp.int32),
            pltpu.VMEM((rows, t_cols), bf16),
            pltpu.VMEM((ab_tiles, TILE, TILE), bf16),
            pltpu.VMEM((n_virt, rows, t_cols), bf16),
            pltpu.VMEM((n_pair, VCAP, TILE, TILE), bf16),
            pltpu.VMEM((VCAP + 1, TILE, TILE), bf16),
            pltpu.VMEM((ab_rows, 2 * TILE), bf16),
            pltpu.VMEM((rows, ab_rows), jnp.float32),
            dma((4,)),
            dma((n_pair, CHUNKS)),
            dma((3, n_pair, CHUNKS)),
            dma((n_virt,)),
            dma((n_virt,)),
            dma((n_virt,)),
        ],
        compiler_params=pltpu.CompilerParams(
            collective_id=0, has_side_effects=True, vmem_limit_bytes=60 * 2**20
        ),
    )(t_mask.T, v_mask, t_amps, v_ints.reshape(ab_tiles, TILE, TILE))


def solution(mesh):
    return jax.shard_map(
        functools.partial(local, mesh.shape["pair"], mesh.shape["virt"]),
        mesh=mesh,
        in_specs=(P("pair", "virt"), P("virt", "pair"), P("pair", "virt"), P("virt", None)),
        out_specs=P("pair", "virt"),
        check_vma=False,
    )
```

```python
import functools

import jax
import jax.numpy as jnp
from jax import lax
from jax.experimental import pallas as pl
from jax.experimental.pallas import tpu as pltpu
from jax.sharding import PartitionSpec as P

TILE = 128
VCAP = 4
CHUNKS = 2
WINDOW = 3
NT = 256
MESH = pl.DeviceIdType.MESH


def nth_nearest(s, z, Z):
    low = jnp.minimum(z, Z - 1 - z)
    near = z - (s + 1) // 2 if s % 2 else z + s // 2
    far = jnp.where(z < Z - 1 - z, s, Z - 1 - s)
    return jnp.where(s <= 2 * low, near, far)


def kernel(
    Z, H, tm_hbm, vm_hbm, t_hbm, v_hbm, out_ref,
    tm_ref, vm_ref, t_in, v_in, tf, vc, stage, vd, acc,
    in_sem, v_recv, v_send, t_recv, t_far, t_near,
):
    ab_tiles = vm_ref.shape[0]
    me = lax.axis_index("pair")
    my_q = lax.axis_index("virt")
    z, x = me // 2, me % 2
    h, c = my_q // 2, my_q % 2
    up, down, side = me + 2, me - 2, 2 * z + (1 - x)
    sibling = 2 * h + (1 - c)

    load_v = pltpu.make_async_copy(v_hbm, v_in, in_sem.at[0])
    load_t = pltpu.make_async_copy(t_hbm, t_in, in_sem.at[1])
    load_vm = pltpu.make_async_copy(vm_hbm, vm_ref, in_sem.at[2])
    load_tm = pltpu.make_async_copy(tm_hbm, tm_ref, in_sem.at[3])
    load_vm.start()
    load_v.start()
    load_tm.start()
    load_t.start()

    barrier = pltpu.get_barrier_semaphore()

    def greet(pair, virt):
        pl.semaphore_signal(barrier, inc=1, device_id=(pair, virt), device_id_type=MESH)

    @pl.when(z > 0)
    def _():
        greet(down, my_q)

    @pl.when(z < Z - 1)
    def _():
        greet(up, my_q)

    greet(side, my_q)
    greet(me, sibling)
    for i in range(1, H):
        greet(me, 2 * lax.rem(h + i, H) + c)

    load_vm.wait()
    seen = jnp.int32(0)
    picks = [jnp.int32(0)] * VCAP
    for i in range(ab_tiles):
        flag = vm_ref[i, me]
        for j in range(VCAP):
            picks[j] = jnp.where((flag != 0) & (seen == j), i, picks[j])
        seen = seen + flag
    load_v.wait()
    for j in range(VCAP):
        vc[me, j] = v_in[picks[j]]

    pl.semaphore_wait(
        barrier,
        1 + H + jnp.where(z > 0, 1, 0) + jnp.where(z < Z - 1, 1, 0),
    )

    def v_copy(block, u, way, to):
        part = pl.ds(u * (VCAP // CHUNKS), VCAP // CHUNKS)
        return pltpu.make_async_remote_copy(
            src_ref=vc.at[block, part],
            dst_ref=vc.at[block, part],
            send_sem=v_send.at[way, block, u],
            recv_sem=v_recv.at[block, u],
            device_id=(to, my_q),
            device_id_type=MESH,
        )

    def t_copy(block, sem, to):
        return pltpu.make_async_remote_copy(
            src_ref=tf.at[block],
            dst_ref=tf.at[block],
            send_sem=sem,
            recv_sem=t_recv.at[block],
            device_id=(me, to),
            device_id_type=MESH,
        )

    def stream(way, s):
        if way == 0:
            return z - s, (z >= s) & (z < Z - 1), up
        if way == 1:
            return z + s, (z + s < Z) & (z > 0), down
        return nth_nearest(s, z, Z), None, side

    def each(way, n, act):
        a, there, to = stream(way, n // CHUNKS)
        copy = v_copy(2 * a + x, n % CHUNKS, way, to)
        if there is None:
            act(copy)
        else:
            pl.when(there)(lambda: act(copy))

    def start(copy):
        copy.start()

    def wait_send(copy):
        copy.wait_send()

    def drain(way, n):
        there = stream(way, n // CHUNKS)[1]
        if there is None:
            if n + WINDOW >= Z * CHUNKS:
                each(way, n, wait_send)
        elif n + WINDOW >= Z * CHUNKS:
            each(way, n, wait_send)
        else:
            later = stream(way, (n + WINDOW) // CHUNKS)[1]

            @pl.when(jnp.logical_not(later))
            def _():
                each(way, n, wait_send)

    def tick(n):
        s, u = n // CHUNKS, n % CHUNKS
        if s > 0:

            @pl.when(z >= s)
            def _():
                v_copy(2 * (z - s) + x, u, 0, side).wait_recv()

            @pl.when(z + s < Z)
            def _():
                v_copy(2 * (z + s) + x, u, 0, side).wait_recv()

        for way in range(3):
            if n >= WINDOW:
                a, there, to = stream(way, s)
                if there is None:
                    each(way, n - WINDOW, wait_send)
                else:
                    pl.when(there)(lambda: each(way, n - WINDOW, wait_send))
            each(way, n, start)

    for n in range(WINDOW):
        tick(n)

    load_tm.wait()
    load_t.wait()
    cd = tm_ref.shape[0]
    for i in range(tm_ref.shape[1]):
        for j in range(cd):
            rows, cols = pl.ds(i * TILE, TILE), pl.ds(j * TILE, TILE)
            flag = jnp.full((TILE, TILE), tm_ref[j, i].astype(jnp.float32))
            tf[my_q, rows, cols] = t_in[rows, cols] * flag.astype(jnp.bfloat16)
    for i in range(1, H):
        t_copy(my_q, t_far.at[i], 2 * lax.rem(h + i, H) + c).start()
    t_copy(my_q, t_near.at[my_q], sibling).start()

    stage[VCAP] = jnp.zeros((TILE, TILE), jnp.bfloat16)

    def expand(a):
        for j in range(2):
            k = 2 * a + j
            for i in range(VCAP):
                stage[i] = vc[k, i]
            rank = jnp.int32(0)
            for i in range(ab_tiles):
                flag = vm_ref[i, k]
                where = jnp.where(flag != 0, rank, VCAP)
                rank = rank + flag
                vd[pl.ds(i * TILE, TILE), pl.ds(j * TILE, TILE)] = stage[where]

    def multiply(a, s):
        expand(a)
        left = tf.at[a]

        @pl.loop(0, ab_tiles * TILE // NT)
        def _(n):
            cols = pl.ds(pl.multiple_of(n * NT, NT), NT)
            part = lax.dot_general(
                left[...], vd[cols, :], (((1,), (1,)), ((), ())),
                preferred_element_type=jnp.float32,
            )
            if s > 0:
                part = part + acc[:, cols]
            if s < Z - 1:
                acc[:, cols] = part
            else:
                out_ref[:, cols] = part.astype(out_ref.dtype)

    def finish(s):
        a = nth_nearest(s, z, Z)
        for u in range(CHUNKS):
            v_copy(2 * a + (1 - x), u, 2, side).wait_recv()
        multiply(a, s)

    def t_onward():
        for i in range(1, H):
            block = 2 * lax.rem(h + H - i, H) + c
            t_copy(block, t_far.at[i], sibling).wait_recv()
            t_copy(block, t_near.at[block], sibling).start()

    def t_arrived():
        for i in range(H):
            block = 2 * i + (1 - c)
            t_copy(block, t_near.at[block], sibling).wait_recv()

    done = 0
    last = (Z - 1) * CHUNKS
    for n in range(WINDOW, Z * CHUNKS):
        tick(n)
        if n == last - 1:
            t_onward()
        if n == last - 0:
            t_arrived()
        if n >= last - 0 and done < Z - 1:
            finish(done)
            done += 1
    for s in range(done, Z):
        finish(s)

    for n in range(Z * CHUNKS):
        for way in range(3):
            drain(way, n)
    for i in range(1, H):
        t_copy(my_q, t_far.at[i], sibling).wait_send()
    for i in range(H):
        block = 2 * i + c
        t_copy(block, t_near.at[block], sibling).wait_send()


def local(n_pair, n_virt, t_amps, v_ints, t_mask, v_mask):
    rows, t_cols = t_amps.shape
    ab_rows, _ = v_ints.shape
    ab_tiles = ab_rows // TILE
    dma = pltpu.SemaphoreType.DMA
    bf16 = jnp.bfloat16
    return pl.pallas_call(
        functools.partial(kernel, n_pair // 2, n_virt // 2),
        out_shape=pltpu.VMEM((rows, ab_rows), bf16),
        in_specs=[pl.BlockSpec(memory_space=pl.ANY)] * 4,
        out_specs=pl.BlockSpec(memory_space=pltpu.VMEM),
        scratch_shapes=[
            pltpu.SMEM(t_mask.shape[::-1], jnp.int32),
            pltpu.SMEM(v_mask.shape, jnp.int32),
            pltpu.VMEM((rows, t_cols), bf16),
            pltpu.VMEM((ab_tiles, TILE, TILE), bf16),
            pltpu.VMEM((n_virt, rows, t_cols), bf16),
            pltpu.VMEM((n_pair, VCAP, TILE, TILE), bf16),
            pltpu.VMEM((VCAP + 1, TILE, TILE), bf16),
            pltpu.VMEM((ab_rows, 2 * TILE), bf16),
            pltpu.VMEM((rows, ab_rows), jnp.float32),
            dma((4,)),
            dma((n_pair, CHUNKS)),
            dma((3, n_pair, CHUNKS)),
            dma((n_virt,)),
            dma((n_virt,)),
            dma((n_virt,)),
        ],
        compiler_params=pltpu.CompilerParams(
            collective_id=0, has_side_effects=True, vmem_limit_bytes=60 * 2**20
        ),
    )(t_mask.T, v_mask, t_amps, v_ints.reshape(ab_tiles, TILE, TILE))


def solution(mesh):
    return jax.shard_map(
        functools.partial(local, mesh.shape["pair"], mesh.shape["virt"]),
        mesh=mesh,
        in_specs=(P("pair", "virt"), P("virt", "pair"), P("pair", "virt"), P("virt", None)),
        out_specs=P("pair", "virt"),
        check_vma=False,
    )
```
